128 devices in a mesh: section: 4 (over y), kv: 32 (over x, z, core).
Axes of the slice: x: 4, y: 4, z: 4, core: 2. Of those that a mesh axis runs over, the one named last changes fastest.
Arguments:
- hidden: bfloat16 [4, 64, 8192], P('section'), may hold values from -6 to 6
- norm_gain: float32 [4, 8192], P('section'), may hold values from 0.1 to 1.9
- query_weight: bfloat16 [4, 8192, 8192], P('section', None, 'kv'), may hold values from -0.0625 to 0.0625
- key_cache: bfloat16 [4, 384, 256, 1024], P('section', 'kv')
- value_cache: bfloat16 [4, 384, 256, 1024], P('section', 'kv'), may hold values from -6 to 6
- out_weight: bfloat16 [4, 8192, 8192], P('section', 'kv'), may hold values from -0.0625 to 0.0625
- block_pos: int32 [384], P('kv'), may hold values from 0 to 383, each once
- lengths: int32 [32], replicated, may hold values from 1 to 98304, as said below
- span_start: int32 [1], replicated, may hold values from 0 to 98272
Outputs:
- next_hidden: bfloat16 [4, 64, 8192], P('section', 'kv')
The draws below stay inside these ranges and needn't reach their ends.
Inputs may be any that keep to these rules, and one draw needn't show every extreme that they name: `block_pos`: every context block index appears in exactly one slot. `lengths`: some decode row reads the whole context.
All inputs are finite; a program needn't handle non-finite values.
Results may differ from the reference program's by a relative error of at most 0.015.
Values may be sent and summed in bfloat16 or wider, within the bound.
A program may use at most 320 MiB of HBM per device.

```python
import jax
import jax.numpy as jnp
from jax import lax

D = 8192
HQ = 64
KVH = 8
HD = 128
BLOCK = 256
PRE = 32
DEC = 32
SECTIONS = 4
NBLK = 384
CTX = 98304


def draw_lengths(key, part):
    key = jax.random.fold_in(key, 11)
    first_key, second_key = jax.random.split(key)
    drawn = jax.random.randint(first_key, (DEC,), 1, CTX + 1, dtype=jnp.int32)
    where_full = jax.random.randint(second_key, (), 0, DEC, dtype=jnp.int32)
    return drawn.at[where_full].set(CTX)


def draw_key_cache(key, part):
    key = jax.random.fold_in(key, 23)
    base_key = jax.random.fold_in(key, 0)
    return jax.random.truncated_normal(base_key, -6.0, 6.0, (SECTIONS, NBLK, BLOCK, KVH * HD), jnp.float32).astype(jnp.bfloat16)


def levels(stream_key, dims, cuts, low, largest):
    loudness, own = 1.0, jax.random.fold_in(stream_key, 6)
    for dim, shards_of in cuts:
        steps = jnp.exp(jax.random.uniform(jax.random.fold_in(own, dim), (shards_of,), jnp.float32, low / len(cuts), largest / len(cuts)))
        loudness = loudness * jnp.repeat(steps, dims[dim] // shards_of).reshape([-1 if axis == dim else 1 for axis in range(len(dims))])
    return loudness


def scatter_about(own_key, dims, scale, reach, cuts=(), kind=jnp.bfloat16):
    loudness = levels(own_key, dims, cuts, -0.22, 0.18) if cuts else 1.0
    result = jax.random.normal(own_key, dims, jnp.float32) * scale * loudness
    return jnp.minimum(jnp.maximum(result, -reach), reach).astype(kind)


def setup_inputs(seed: int = 0) -> dict:
    arg_keys = jax.random.split(jax.random.key(seed), 10)
    return {
        "hidden": scatter_about(arg_keys[0], (SECTIONS, PRE + DEC, D), 1.0, 6.0, ((0, 4),)),
        "norm_gain": jnp.clip(1.0 + 0.18 * jax.random.normal(arg_keys[1], (SECTIONS, D), jnp.float32), 0.1, 1.9),
        "query_weight": scatter_about(arg_keys[2], (SECTIONS, D, HQ * HD), D ** -0.5, 0.0625, ((0, 4), (2, 32))),
        "key_cache": draw_key_cache(jax.random.fold_in(arg_keys[9], 71), 0),
        "value_cache": scatter_about(arg_keys[4], (SECTIONS, NBLK, BLOCK, KVH * HD), 1.0, 6.0, ((0, 4), (1, 32))),
        "out_weight": scatter_about(arg_keys[5], (SECTIONS, HQ * HD, D), (HQ * HD) ** -0.5, 0.0625, ((0, 4), (1, 32))),
        "block_pos": jax.random.permutation(arg_keys[6], NBLK).astype(jnp.int32),
        "lengths": draw_lengths(jax.random.fold_in(arg_keys[9], 71), 0),
        "span_start": jax.random.randint(arg_keys[8], (1,), 0, CTX - PRE + 1).astype(jnp.int32),
    }


def attend_head(query_group, key_head, value_head, allowed):
    scores = jnp.einsum('rgd,cd->rgc', query_group.astype(jnp.float32), key_head.astype(jnp.float32)) * HD ** (-0.5)
    masked = jnp.where(allowed[:, None, :], scores, jnp.float32(-1e+30))
    peak = lax.optimization_barrier(jnp.max(masked, axis=2, keepdims=True))
    weights = jnp.where(allowed[:, None, :], jnp.exp(scores - peak), jnp.float32(0.0))
    total = lax.optimization_barrier(jnp.sum(weights, axis=2))
    rounded = weights.astype(jnp.bfloat16)
    summed = jnp.einsum('rgc,cd->rgd', rounded.astype(jnp.float32), value_head.astype(jnp.float32))
    return summed / total[..., None]

def reference(hidden, norm_gain, query_weight, key_cache, value_cache, out_weight, block_pos, lengths, span_start):
    row_count = PRE + DEC
    group = HQ // KVH
    positions = (block_pos[:, None] * BLOCK + jnp.arange(BLOCK, dtype=jnp.int32)[None, :]).reshape(-1)
    limits = jnp.concatenate([span_start[0] + jnp.arange(PRE, dtype=jnp.int32) + 1, lengths.astype(jnp.int32)])
    allowed = positions[None, :] < limits[:, None]
    results = []
    for section_id in range(SECTIONS):
        states = hidden[section_id].astype(jnp.float32)
        scale = lax.rsqrt(lax.optimization_barrier(jnp.mean(states * states, axis=1, keepdims=True)) + 1e-05)
        normed = (states * scale * norm_gain[section_id][None, :]).astype(jnp.bfloat16)
        queries = jnp.dot(normed, query_weight[section_id], preferred_element_type=jnp.float32).astype(jnp.bfloat16)
        query_heads = jnp.moveaxis(queries.reshape(row_count, KVH, group, HD), 1, 0)
        key_heads = jnp.moveaxis(key_cache[section_id].reshape(NBLK * BLOCK, KVH, HD), 1, 0)
        value_heads = jnp.moveaxis(value_cache[section_id].reshape(NBLK * BLOCK, KVH, HD), 1, 0)

        def per_head(operands):
            return attend_head(operands[0], operands[1], operands[2], allowed)
        attended = lax.map(per_head, (query_heads, key_heads, value_heads))
        attended = jnp.moveaxis(attended, 0, 1).reshape(row_count, HQ * HD).astype(jnp.bfloat16)
        projected = jnp.dot(attended, out_weight[section_id], preferred_element_type=jnp.float32)
        results.append((states + projected).astype(jnp.bfloat16))
    stacked = jnp.stack(results)
    return jnp.roll(stacked, 1, axis=0)
```

```python
import functools
import math

import jax
import jax.numpy as jnp
from jax import lax
from jax.experimental import pallas as pl
from jax.experimental.pallas import tpu as pltpu
from jax.sharding import PartitionSpec as P

HD = 128
LOG2_SCALE = math.log2(math.e) / math.sqrt(HD)
HIDDEN_BY_MASK = -1e30
PEAK_FLOOR = -1e28
MESH = pl.DeviceIdType.MESH
BF16, F32, I32 = jnp.bfloat16, jnp.float32, jnp.int32


def dot(a, b, contract=((1,), (0,))):
    return lax.dot_general(a, b, (contract, ((), ())), preferred_element_type=F32)


def arrived(ref, sem):
    pltpu.make_async_copy(ref, ref, sem).wait()


def kernel(
    sections,
    kv_count,
    hid_h,
    gain_h,
    wq_h,
    key_h,
    value_h,
    wo_h,
    block_pos,
    lengths,
    span_start,
    out,
    hid,
    gain,
    wq,
    keys,
    values,
    wo,
    queries,
    onehot,
    bias,
    blocks,
    q_out,
    o_out,
    stat_out,
    o_in,
    stat_in,
    attended,
    acc,
    rs_out,
    rs_in,
    fin_out,
    fin_in,
    in_sem,
    wq_sem,
    own_sem,
    kv_send,
    kv_recv,
    block_sem,
    q_send,
    q_recv,
    o_send,
    o_recv,
    stat_send,
    stat_recv,
    att_sem,
    rs_send,
    rs_recv,
    fin_send,
    fin_recv,
):
    rows, width = hid.shape
    x_count = kv_count // 8
    chips = kv_count // 2
    slots, block = key_h.shape[1], key_h.shape[2]
    half = width // 2
    lanes = rs_out.shape[2]
    span = slots * block
    section = lax.axis_index("section")
    me = lax.axis_index("kv")
    chip = lax.div(me, 2)
    core = lax.rem(me, 2)
    other = 1 - core
    sibling = chip * 2 + other
    x = lax.div(chip, 4)
    z = lax.rem(chip, 4)
    side = lax.div(z, 2)
    place = lax.rem(z, 2) * 2 + core

    load_hid = pltpu.make_async_copy(hid_h.at[0], hid, in_sem.at[0])
    load_gain = pltpu.make_async_copy(gain_h, gain, in_sem.at[1])
    load_hid.start()
    load_gain.start()
    pieces = wq_sem.shape[0]
    deep = wq.shape[0] // pieces

    def load_wq(n):
        part = pl.ds(n * deep, deep)
        return pltpu.make_async_copy(wq_h.at[0, part], wq.at[part], wq_sem.at[n])

    for n in range(pieces):
        load_wq(n).start()

    barrier = pltpu.get_barrier_semaphore()

    def greet(n, carry):
        @pl.when(n != me)
        def _():
            pl.semaphore_signal(barrier, inc=1, device_id={"kv": n}, device_id_type=MESH)

        return carry

    lax.fori_loop(0, kv_count, greet, 0)
    after = lax.rem(section + 1, sections)
    before = lax.rem(section + sections - 1, sections)
    for there in (after, before):
        for c in range(2):
            pl.semaphore_signal(
                barrier,
                inc=1,
                device_id={"section": there, "kv": chip * 2 + c},
                device_id_type=MESH,
            )

    blocks[0] = jnp.zeros((16, 128), F32)
    for j in range(slots):
        blocks[0, j : j + 1, :] = jnp.full((1, 128), block_pos[j], I32).astype(F32)
    lane = lax.broadcasted_iota(I32, (1, 128), 1)
    prefill = rows - lengths.shape[0]
    limits = span_start[0] + lane + 1
    for r in range(lengths.shape[0]):
        limits = jnp.where(lane == prefill + r, lengths[r], limits)
    limits = limits.astype(F32)
    token = lax.broadcasted_iota(I32, (block, 128), 0).astype(F32)

    def mask_columns(which):
        for j in range(slots):
            position = blocks[which, j : j + 1, :] * float(block) + token
            bias[pl.ds((which * slots + j) * block, block), :] = jnp.where(
                position < limits, 0.0, HIDDEN_BY_MASK
            ).astype(BF16)

    mask_columns(0)
    wide = onehot.shape[0]
    onehot[...] = jnp.where(
        lax.rem(lax.broadcasted_iota(I32, (wide, 128), 0), rows)
        == lax.broadcasted_iota(I32, (wide, 128), 1),
        1.0,
        0.0,
    ).astype(BF16)

    pl.semaphore_wait(barrier, kv_count - 1 + 4)

    def to_sibling(src, dst, n):
        return pltpu.make_async_remote_copy(
            src_ref=src,
            dst_ref=dst,
            send_sem=kv_send.at[n],
            recv_sem=kv_recv.at[n],
            device_id={"kv": sibling},
            device_id_type=MESH,
        )

    def head_at(i):
        return lax.rem(x + i, x_count)

    def head_lanes(slot, c):
        return pl.ds(pl.multiple_of((slot * 2 + c) * HD, HD), HD)

    def swap_copies():
        copies = []
        for i in range(x_count):
            slot = head_at(i)
            for k, (src, dst) in enumerate(((key_h, keys), (value_h, values))):
                copies.append(
                    to_sibling(
                        src.at[0, :, :, head_lanes(slot, other)],
                        dst.at[slot, pl.ds(slots, slots)],
                        i * 2 + k,
                    )
                )
        copies.append(
            to_sibling(
                wo_h.at[0, :, pl.ds(pl.multiple_of(other * half, half), half)],
                wo.at[core],
                2 * x_count,
            )
        )
        return copies

    send_blocks = pltpu.make_async_remote_copy(
        src_ref=blocks.at[0],
        dst_ref=blocks.at[1],
        send_sem=block_sem.at[0],
        recv_sem=block_sem.at[1],
        device_id={"kv": sibling},
        device_id_type=MESH,
    )
    send_blocks.start()
    for copy in swap_copies():
        copy.start()

    def own_copies():
        copies = []
        for i in range(x_count):
            slot = head_at(i)
            for k, (src, dst) in enumerate(((key_h, keys), (value_h, values))):
                copies.append(
                    pltpu.make_async_copy(
                        src.at[0, :, :, head_lanes(slot, core)],
                        dst.at[slot, pl.ds(0, slots)],
                        own_sem.at[i * 2 + k],
                    )
                )
        copies.append(
            pltpu.make_async_copy(
                wo_h.at[0, :, pl.ds(pl.multiple_of(core * half, half), half)],
                wo.at[core],
                own_sem.at[2 * x_count],
            )
        )
        return copies

    load_hid.wait()
    load_gain.wait()
    step = min(1024, deep)
    squares = jnp.zeros((rows, 1), F32)
    for n in range(width // step):
        part = hid[:, n * step : (n + 1) * step].astype(F32)
        squares = squares + jnp.sum(part * part, axis=1, keepdims=True)
    scale = lax.rsqrt(squares / width + 1e-05)
    projected = jnp.zeros((rows, 2 * HD), F32)
    for n in range(width // step):
        if n * step % deep == 0:
            load_wq(n * step // deep).wait()
        part = pl.ds(n * step, step)
        normed = (hid[:, part].astype(F32) * scale * gain[:, part]).astype(BF16)
        projected = projected + dot(normed, wq[part, :])
    q_out[pl.ds(0, rows), :] = projected[:, :HD].astype(BF16)
    q_out[pl.ds(rows, rows), :] = projected[:, HD:].astype(BF16)

    pair = 2 * rows

    def q_target(n):
        to_x = lax.rem(x + x_count - lax.div(n, 4), x_count)
        to_z = lax.rem(z + n, 4)
        return to_x * 8 + to_z * 2 + side

    def q_place():
        return queries.at[x, pl.ds(pl.multiple_of(place * pair, pair), pair)]

    def q_copy(n):
        return pltpu.make_async_remote_copy(
            src_ref=q_out,
            dst_ref=q_place(),
            send_sem=q_send.at[n],
            recv_sem=q_recv.at[x * 4 + place],
            device_id={"kv": q_target(n)},
            device_id_type=MESH,
        )

    def send_queries(n, carry):
        @pl.when(q_target(n) != me)
        def _():
            q_copy(n).start()

        @pl.when(q_target(n) == me)
        def _():
            pltpu.make_async_copy(q_out, q_place(), q_recv.at[x * 4 + place]).start()

        return carry

    lax.fori_loop(0, x_count * 4, send_queries, 0)
    for copy in own_copies():
        copy.start()
    arrived(blocks.at[1], block_sem.at[1])
    mask_columns(1)

    def o_target(slot, p):
        return slot * 8 + (core * 2 + p // 2) * 2 + p % 2

    def o_copies(i, p):
        slot = head_at(i)
        n = i * 4 + p
        return tuple(
            pltpu.make_async_remote_copy(
                src_ref=src.at[slot, p],
                dst_ref=dst.at[chip],
                send_sem=send.at[n],
                recv_sem=recv.at[chip],
                device_id={"kv": o_target(slot, p)},
                device_id_type=MESH,
            )
            for src, dst, send, recv in (
                (o_out, o_in, o_send, o_recv),
                (stat_out, stat_in, stat_send, stat_recv),
            )
        )

    def attend(i, carry):
        slot = head_at(i)
        for p in range(4):
            arrived(queries.at[slot, pl.ds(p * pair, pair)], q_recv.at[slot * 4 + p])
        for k, held in enumerate((keys, values)):
            arrived(held.at[slot, pl.ds(0, slots)], own_sem.at[i * 2 + k])
            arrived(held.at[slot, pl.ds(slots, slots)], kv_recv.at[i * 2 + k])
        query = jnp.concatenate([queries[slot], onehot[...]], axis=1)

        def scores_of(n):
            key = keys[slot, pl.ds(n * slots, slots)].reshape(span, HD)
            key = jnp.concatenate([key, bias[pl.ds(n * span, span), :]], axis=1)
            return dot(key, query, ((1,), (1,)))

        peak = jnp.full((8, wide), PEAK_FLOOR, F32)
        total = jnp.zeros((8, wide), F32)
        summed = jnp.zeros((HD, wide), F32)
        scores = scores_of(0)
        for n in range(2):
            coming = scores_of(1) if n == 0 else None
            scores = scores.reshape(span // 8, 8, wide)
            largest = jnp.max(jnp.max(scores, axis=0), axis=0, keepdims=True)
            new_peak = jnp.maximum(peak, largest)
            decay = jnp.exp2((peak - new_peak) * LOG2_SCALE)
            weights = jnp.exp2(scores * LOG2_SCALE - (new_peak * LOG2_SCALE)[None])
            total = total * decay + jnp.sum(weights, axis=0)
            weights = weights.reshape(span, wide).astype(BF16)
            value = values[slot, pl.ds(n * slots, slots)].reshape(span, HD)
            summed = summed * decay[0:1] + dot(value, weights, ((0,), (0,)))
            peak = new_peak
            scores = coming
        total = jnp.sum(total, axis=0, keepdims=True)
        for p in range(4):
            part = slice(p * pair, (p + 1) * pair)
            o_out[slot, p] = summed[:, part].astype(BF16)
            stat_out[slot, p] = jnp.concatenate(
                [peak[0:4, part], jnp.broadcast_to(total[:, part], (4, pair))], axis=0
            )
        for p in range(4):

            @pl.when(o_target(slot, p) != me)
            def _():
                for copy in o_copies(i, p):
                    copy.start()

            @pl.when(o_target(slot, p) == me)
            def _():
                pltpu.make_async_copy(o_out.at[slot, p], o_in.at[chip], o_recv.at[chip]).start()
                pltpu.make_async_copy(
                    stat_out.at[slot, p], stat_in.at[chip], stat_recv.at[chip]
                ).start()

        return carry

    lax.fori_loop(0, x_count, attend, 0)

    def await_sums(n, carry):
        arrived(o_in.at[n], o_recv.at[n])
        arrived(stat_in.at[n], stat_recv.at[n])
        return carry

    lax.fori_loop(0, chips, await_sums, 0)
    peaks = stat_in[:, 0, :]
    totals = stat_in[:, 4, :]
    share = jnp.exp2((peaks - jnp.max(peaks, axis=0, keepdims=True)) * LOG2_SCALE)
    share = share / jnp.sum(share * totals, axis=0, keepdims=True)
    joined = jnp.zeros((HD, pair), F32)
    for n in range(chips):
        joined = joined + share[n : n + 1] * o_in[n].astype(F32)
    joined = joined.T.astype(BF16)
    attended[core] = jnp.concatenate([joined[:rows], joined[rows:]], axis=1)
    share_heads = pltpu.make_async_remote_copy(
        src_ref=attended.at[core],
        dst_ref=attended.at[core],
        send_sem=att_sem.at[0],
        recv_sem=att_sem.at[1],
        device_id={"kv": sibling},
        device_id_type=MESH,
    )
    share_heads.start()

    def spread(count, first, q):
        at = lax.broadcasted_iota(I32, (count, rows), 0)
        row = (at // 16) * 4 + ((at // 8) % 2) * 2 + at % 2 + first
        hit = (row == lax.broadcasted_iota(I32, (count, rows), 1)) & ((at // 2) % 4 == q)
        return jnp.where(hit, 1.0, 0.0).astype(BF16)

    strip = min(512, lanes)

    def project(c):
        parts = [dot(spread(16 * chips, 0, q), attended[c]).astype(BF16) for q in range(4)]
        for n in range(lanes // strip):
            total = None
            for q in range(4):
                term = dot(parts[q], wo[c, :, pl.ds(q * lanes + n * strip, strip)])
                total = term if total is None else total + term
            yield pl.ds(n * strip, strip), total

    arrived(wo.at[core], own_sem.at[2 * x_count])
    for part, term in project(core):
        acc[:, part] = term
    arrived(wo.at[other], kv_recv.at[2 * x_count])
    arrived(attended.at[other], att_sem.at[1])
    for part, term in project(other):
        rs_out[:, :, part] = (acc[:, part] + term).astype(BF16).reshape(chips, 16, strip)

    def rs_copy(n):
        to = lax.rem(chip + n, chips)
        return pltpu.make_async_remote_copy(
            src_ref=rs_out.at[to],
            dst_ref=rs_in.at[chip],
            send_sem=rs_send.at[n],
            recv_sem=rs_recv.at[chip],
            device_id={"kv": to * 2 + core},
            device_id_type=MESH,
        )

    def send_terms(n, carry):
        rs_copy(n).start()
        return carry

    lax.fori_loop(1, chips, send_terms, 0)

    result = rs_out[chip].astype(F32)
    for q in range(4):
        own = hid[:, pl.ds(pl.multiple_of(core * half + q * lanes, lanes), lanes)]
        result = result + dot(spread(16, chip * 4, q), own)

    def add_term(n, total):
        source = lax.rem(chip + n, chips)
        arrived(rs_in.at[source], rs_recv.at[source])
        return total + rs_in[source].astype(F32)

    result = lax.fori_loop(1, chips, add_term, result)

    def fin_copy(c):
        return pltpu.make_async_remote_copy(
            src_ref=fin_out.at[c],
            dst_ref=fin_in.at[core],
            send_sem=fin_send.at[c],
            recv_sem=fin_recv.at[core],
            device_id={"section": after, "kv": chip * 2 + c},
            device_id_type=MESH,
        )

    for c in range(2):
        mine = result[8 * c : 8 * c + 8]
        fin_out[c] = jnp.concatenate(
            [mine[:, : lanes // 2], mine[:, lanes // 2 :]], axis=0
        ).astype(BF16)
        fin_copy(c).start()
    for c in range(2):
        arrived(fin_in.at[c], fin_recv.at[c])
    out[...] = fin_in[...]

    send_blocks.wait_send()
    for copy in swap_copies():
        copy.wait_send()

    def queries_left(n, carry):
        @pl.when(q_target(n) != me)
        def _():
            q_copy(n).wait_send()

        return carry

    lax.fori_loop(0, x_count * 4, queries_left, 0)

    def sums_left(i, carry):
        for p in range(4):

            @pl.when(o_target(head_at(i), p) != me)
            def _():
                for copy in o_copies(i, p):
                    copy.wait_send()

        return carry

    lax.fori_loop(0, x_count, sums_left, 0)
    share_heads.wait_send()

    def terms_left(n, carry):
        rs_copy(n).wait_send()
        return carry

    lax.fori_loop(1, chips, terms_left, 0)
    for c in range(2):
        fin_copy(c).wait_send()


def local(sections, kv_count, *args):
    hidden, _, query_weight, key_cache = args[:4]
    rows, width = hidden.shape[1:]
    slots, block = key_cache.shape[1:3]
    x_count, chips = kv_count // 8, kv_count // 2
    pair, wide = 2 * rows, 8 * rows
    lanes = width // 8
    dma = pltpu.SemaphoreType.DMA
    anywhere = pl.BlockSpec(memory_space=pl.ANY)
    scalars = pl.BlockSpec(memory_space=pltpu.SMEM)
    pieces = 4
    out = pl.pallas_call(
        functools.partial(kernel, sections, kv_count),
        out_shape=jax.ShapeDtypeStruct((2, 16, lanes // 2), BF16),
        in_specs=[anywhere] * 6 + [scalars] * 3,
        out_specs=pl.BlockSpec(memory_space=pltpu.VMEM),
        scratch_shapes=[
            pltpu.VMEM((rows, width), BF16),
            pltpu.VMEM((1, width), F32),
            pltpu.VMEM((width, 2 * HD), BF16),
            pltpu.VMEM((x_count, 2 * slots, block, HD), BF16),
            pltpu.VMEM((x_count, 2 * slots, block, HD), BF16),
            pltpu.VMEM((2, 2 * HD, width // 2), BF16),
            pltpu.VMEM((x_count, wide, HD), BF16),
            pltpu.VMEM((wide, 128), BF16),
            pltpu.VMEM((2 * slots * block, 128), BF16),
            pltpu.VMEM((2, 16, 128), F32),
            pltpu.VMEM((pair, HD), BF16),
            pltpu.VMEM((x_count, 4, HD, pair), BF16),
            pltpu.VMEM((x_count, 4, 8, pair), F32),
            pltpu.VMEM((chips, HD, pair), BF16),
            pltpu.VMEM((chips, 8, pair), F32),
            pltpu.VMEM((2, rows, 2 * HD), BF16),
            pltpu.VMEM((16 * chips, lanes), F32),
            pltpu.VMEM((chips, 16, lanes), BF16),
            pltpu.VMEM((chips, 16, lanes), BF16),
            pltpu.VMEM((2, 16, lanes // 2), BF16),
            pltpu.VMEM((2, 16, lanes // 2), BF16),
            dma((2,)),
            dma((pieces,)),
            dma((2 * x_count + 1,)),
            dma((2 * x_count + 1,)),
            dma((2 * x_count + 1,)),
            dma((2,)),
            dma((4 * x_count,)),
            dma((4 * x_count,)),
            dma((4 * x_count,)),
            dma((chips,)),
            dma((4 * x_count,)),
            dma((chips,)),
            dma((2,)),
            dma((chips,)),
            dma((chips,)),
            dma((2,)),
            dma((2,)),
        ],
        compiler_params=pltpu.CompilerParams(
            collective_id=0, has_side_effects=True, vmem_limit_bytes=60 << 20
        ),
        name="relay_attention",
    )(*args)
    out = out.reshape(2, 2, 4, 2, lanes // 2).transpose(3, 0, 2, 1, 4)
    return out.reshape(1, 2, width)


def solution(mesh):
    placed = (
        P("section", None, None),
        P("section", None),
        P("section", None, "kv"),
        P("section", "kv", None, None),
        P("section", "kv", None, None),
        P("section", "kv", None),
        P("kv"),
        P(),
        P(),
    )
    sections, kv_count = mesh.shape["section"], mesh.shape["kv"]
    return jax.shard_map(
        functools.partial(local, sections, kv_count),
        mesh=mesh,
        in_specs=placed,
        out_specs=P("section", "kv", None),
        check_vma=False,
    )
```

```python
import functools
import math

import jax
import jax.numpy as jnp
from jax import lax
from jax.experimental import pallas as pl
from jax.experimental.pallas import tpu as pltpu
from jax.sharding import PartitionSpec as P

HD = 128
LOG2_SCALE = math.log2(math.e) / math.sqrt(HD)
HIDDEN_BY_MASK = -1e30
PEAK_FLOOR = -1e28
MESH = pl.DeviceIdType.MESH
BF16, F32, I32 = jnp.bfloat16, jnp.float32, jnp.int32


def dot(a, b, contract=((1,), (0,))):
    return lax.dot_general(a, b, (contract, ((), ())), preferred_element_type=F32)


def arrived(ref, sem):
    pltpu.make_async_copy(ref, ref, sem).wait()


def kernel(
    sections,
    kv_count,
    hid_h,
    gain_h,
    wq_h,
    key_h,
    value_h,
    wo_h,
    block_pos_h,
    lengths_h,
    span_start_h,
    out,
    block_pos,
    lengths,
    span_start,
    hid,
    gain,
    wq,
    keys,
    values,
    wo,
    queries,
    onehot,
    bias,
    blocks,
    scores,
    q_out,
    o_out,
    stat_out,
    o_in,
    stat_in,
    attended,
    acc,
    rs_out,
    rs_in,
    fin_out,
    fin_in,
    in_sem,
    wq_sem,
    own_sem,
    kv_send,
    kv_recv,
    block_sem,
    q_send,
    q_recv,
    o_send,
    o_recv,
    stat_send,
    stat_recv,
    att_sem,
    rs_send,
    rs_recv,
    fin_send,
    fin_recv,
):
    rows, width = hid.shape
    x_count = kv_count // 8
    chips = kv_count // 2
    slots, block = key_h.shape[1], key_h.shape[2]
    half = width // 2
    lanes = rs_out.shape[2]
    strips = rs_send.shape[0]
    strip = lanes // strips
    span = slots * block
    wide = onehot.shape[0]
    pair = 2 * rows
    section = lax.axis_index("section")
    me = lax.axis_index("kv")
    chip = lax.div(me, 2)
    core = lax.rem(me, 2)
    other = 1 - core
    sibling = chip * 2 + other
    x = lax.div(chip, 4)
    z = lax.rem(chip, 4)
    side = lax.div(z, 2)
    place = core * 2 + lax.rem(z, 2)

    load_hid = pltpu.make_async_copy(hid_h.at[0], hid, in_sem.at[0])
    load_gain = pltpu.make_async_copy(gain_h, gain, in_sem.at[1])
    load_hid.start()
    load_gain.start()
    pieces = wq_sem.shape[0]
    deep = wq.shape[0] // pieces

    def load_wq(n):
        part = pl.ds(n * deep, deep)
        return pltpu.make_async_copy(wq_h.at[0, part], wq.at[part], wq_sem.at[n])

    for n in range(pieces):
        load_wq(n).start()
    scalar_loads = [
        pltpu.make_async_copy(src, dst, in_sem.at[2 + n])
        for n, (src, dst) in enumerate(
            ((block_pos_h, block_pos), (lengths_h, lengths), (span_start_h, span_start))
        )
    ]
    for load in scalar_loads:
        load.start()

    barrier = pltpu.get_barrier_semaphore()

    def greet(n, carry):
        @pl.when(n != me)
        def _():
            pl.semaphore_signal(barrier, inc=1, device_id={"kv": n}, device_id_type=MESH)

        return carry

    lax.fori_loop(0, kv_count, greet, 0)
    after = lax.rem(section + 1, sections)
    before = lax.rem(section + sections - 1, sections)
    for there in (after, before):
        for c in range(2):
            pl.semaphore_signal(
                barrier,
                inc=1,
                device_id={"section": there, "kv": chip * 2 + c},
                device_id_type=MESH,
            )

    load_hid.wait()
    load_gain.wait()
    step = min(1024, deep)
    squares = jnp.zeros((rows, 1), F32)
    for n in range(width // step):
        part = hid[:, n * step : (n + 1) * step].astype(F32)
        squares = squares + jnp.sum(part * part, axis=1, keepdims=True)
    scale = lax.rsqrt(squares / width + 1e-05)
    projected = jnp.zeros((rows, 2 * HD), F32)
    for n in range(width // step):
        if n * step % deep == 0:
            load_wq(n * step // deep).wait()
        part = pl.ds(n * step, step)
        normed = (hid[:, part].astype(F32) * scale * gain[:, part]).astype(BF16)
        projected = projected + dot(normed, wq[part, :])
    projected = projected * LOG2_SCALE
    q_out[pl.ds(0, rows), :] = projected[:, :HD].astype(BF16)
    q_out[pl.ds(rows, rows), :] = projected[:, HD:].astype(BF16)

    def moved(i, at_z):
        return lax.rem((i + 1) * jnp.where(lax.rem(at_z, 2) == 0, 1, x_count - 1), x_count)

    def head_at(i):
        return lax.rem(x + moved(i, z), x_count)

    def head_lanes(slot, c):
        return pl.ds(pl.multiple_of((slot * 2 + c) * HD, HD), HD)

    def own_copies():
        copies = []
        for i in range(x_count):
            slot = head_at(i)
            for k, (src, dst) in enumerate(((key_h, keys), (value_h, values))):
                copies.append(
                    pltpu.make_async_copy(
                        src.at[0, :, :, head_lanes(slot, core)],
                        dst.at[slot, pl.ds(0, slots)],
                        own_sem.at[i * 2 + k],
                    )
                )
        copies.append(
            pltpu.make_async_copy(
                wo_h.at[0, :, pl.ds(pl.multiple_of(core * half, half), half)],
                wo.at[core],
                own_sem.at[2 * x_count],
            )
        )
        return copies

    def to_sibling(src, dst, n):
        return pltpu.make_async_remote_copy(
            src_ref=src,
            dst_ref=dst,
            send_sem=kv_send.at[n],
            recv_sem=kv_recv.at[n],
            device_id={"kv": sibling},
            device_id_type=MESH,
        )

    def swap_copies():
        copies = []
        for i in range(x_count):
            slot = head_at(i)
            for k, (src, dst) in enumerate(((key_h, keys), (value_h, values))):
                copies.append(
                    to_sibling(
                        src.at[0, :, :, head_lanes(slot, other)],
                        dst.at[slot, pl.ds(slots, slots)],
                        i * 2 + k,
                    )
                )
        copies.append(
            to_sibling(
                wo_h.at[0, :, pl.ds(pl.multiple_of(other * half, half), half)],
                wo.at[core],
                2 * x_count,
            )
        )
        return copies

    for copy in own_copies():
        copy.start()
    pl.semaphore_wait(barrier, kv_count - 1 + 4)

    def q_target(n):
        to_z = lax.rem(z + n, 4)
        to_x = lax.rem(x + x_count - moved(lax.div(n, 4), to_z), x_count)
        return to_x * 8 + to_z * 2 + side

    def q_place():
        return queries.at[x, pl.ds(pl.multiple_of(place * pair, pair), pair)]

    def q_copy(n):
        return pltpu.make_async_remote_copy(
            src_ref=q_out,
            dst_ref=q_place(),
            send_sem=q_send.at[n],
            recv_sem=q_recv.at[x * 4 + place],
            device_id={"kv": q_target(n)},
            device_id_type=MESH,
        )

    def send_queries(n, carry):
        @pl.when(q_target(n) != me)
        def _():
            q_copy(n).start()

        @pl.when(q_target(n) == me)
        def _():
            pltpu.make_async_copy(q_out, q_place(), q_recv.at[x * 4 + place]).start()

        return carry

    lax.fori_loop(0, 4, send_queries, 0)

    for load in scalar_loads:
        load.wait()
    blocks[0] = jnp.zeros((16, 128), F32)
    for j in range(slots):
        blocks[0, j : j + 1, :] = jnp.full((1, 128), block_pos[j], I32).astype(F32)
    send_blocks = pltpu.make_async_remote_copy(
        src_ref=blocks.at[0],
        dst_ref=blocks.at[1],
        send_sem=block_sem.at[0],
        recv_sem=block_sem.at[1],
        device_id={"kv": sibling},
        device_id_type=MESH,
    )
    send_blocks.start()
    for copy in swap_copies():
        copy.start()
    lane = lax.broadcasted_iota(I32, (1, 128), 1)
    prefill = rows - lengths.shape[0]
    limits = span_start[0] + lane + 1
    for r in range(lengths.shape[0]):
        limits = jnp.where(lane == prefill + r, lengths[r], limits)
    limits = limits.astype(F32)
    token = lax.broadcasted_iota(I32, (block, 128), 0).astype(F32)

    def mask_columns(which):
        for j in range(slots):
            position = blocks[which, j : j + 1, :] * float(block) + token
            bias[pl.ds((which * slots + j) * block, block), :] = jnp.where(
                position < limits, 0.0, HIDDEN_BY_MASK
            ).astype(BF16)

    mask_columns(0)
    onehot[...] = jnp.where(
        lax.rem(lax.broadcasted_iota(I32, (wide, 128), 0), rows)
        == lax.broadcasted_iota(I32, (wide, 128), 1),
        1.0,
        0.0,
    ).astype(BF16)
    arrived(blocks.at[1], block_sem.at[1])
    mask_columns(1)
    if x_count > 1:
        lax.fori_loop(4, 8, send_queries, 0)

    def o_target(slot, p):
        return slot * 8 + (core * 2 + p % 2) * 2 + p // 2

    def o_copies(i, p):
        slot = head_at(i)
        n = i * 4 + p
        return tuple(
            pltpu.make_async_remote_copy(
                src_ref=src.at[slot, p],
                dst_ref=dst.at[chip],
                send_sem=send.at[n],
                recv_sem=recv.at[chip],
                device_id={"kv": o_target(slot, p)},
                device_id_type=MESH,
            )
            for src, dst, send, recv in (
                (o_out, o_in, o_send, o_recv),
                (stat_out, stat_in, stat_send, stat_recv),
            )
        )

    def await_first(i):
        slot = head_at(i)
        for p in range(4):
            arrived(queries.at[slot, pl.ds(p * pair, pair)], q_recv.at[slot * 4 + p])
        arrived(keys.at[slot, pl.ds(0, slots)], own_sem.at[i * 2])

    def score(i, n):
        slot = head_at(i)
        query = jnp.concatenate([queries[slot], onehot[...]], axis=1)
        key = keys[slot, pl.ds(n * slots, slots)].reshape(span, HD)
        key = jnp.concatenate([key, bias[pl.ds(n * span, span), :]], axis=1)
        scores[n] = dot(key, query, ((1,), (1,)))

    def weigh(i, n, state, columns):
        peak, total, summed = state
        part = scores[n, :, columns].reshape(span // 8, 8, peak.shape[1])
        largest = jnp.max(jnp.max(part, axis=0), axis=0, keepdims=True)
        new_peak = jnp.maximum(peak, largest)
        decay = jnp.exp2(peak - new_peak)
        weights = jnp.exp2(part - new_peak[None])
        total = total * decay + jnp.sum(weights, axis=0)
        weights = weights.reshape(span, peak.shape[1]).astype(BF16)
        value = values[head_at(i), pl.ds(n * slots, slots)].reshape(span, HD)
        summed = summed * decay[0:1] + dot(value, weights, ((0,), (0,)))
        return new_peak, total, summed

    def attend(i, last):
        slot = head_at(i)
        arrived(values.at[slot, pl.ds(0, slots)], own_sem.at[i * 2 + 1])
        arrived(keys.at[slot, pl.ds(slots, slots)], kv_recv.at[i * 2])
        score(i, 1)
        state = (
            jnp.full((8, wide), PEAK_FLOOR, F32),
            jnp.zeros((8, wide), F32),
            jnp.zeros((HD, wide), F32),
        )
        state = weigh(i, 0, state, pl.ds(0, wide))
        arrived(values.at[slot, pl.ds(slots, slots)], kv_recv.at[i * 2 + 1])
        if not last:
            await_first(i + 1)
            score(i + 1, 0)
        cuts = 2 if last else 1
        for cut in range(cuts):
            size = wide // cuts
            columns = slice(cut * size, (cut + 1) * size)
            peak, total, summed = weigh(
                i, 1, [value[:, columns] for value in state], pl.ds(cut * size, size)
            )
            total = jnp.sum(total, axis=0, keepdims=True)
            owners = range(cut * 4 // cuts, (cut + 1) * 4 // cuts)
            for p in owners:
                part = slice(p * pair - cut * size, (p + 1) * pair - cut * size)
                o_out[slot, p] = summed[:, part].astype(BF16)
                stat_out[slot, p] = jnp.concatenate(
                    [peak[0:4, part], jnp.broadcast_to(total[:, part], (4, pair))], axis=0
                )
            for p in owners:

                @pl.when(o_target(slot, p) != me)
                def _():
                    for copy in o_copies(i, p):
                        copy.start()

                @pl.when(o_target(slot, p) == me)
                def _():
                    pltpu.make_async_copy(
                        o_out.at[slot, p], o_in.at[chip], o_recv.at[chip]
                    ).start()
                    pltpu.make_async_copy(
                        stat_out.at[slot, p], stat_in.at[chip], stat_recv.at[chip]
                    ).start()

    def attend_inner(i, carry):
        attend(i, False)
        return carry

    await_first(0)
    score(0, 0)
    if x_count > 2:
        lax.fori_loop(8, x_count * 4, send_queries, 0)
    lax.fori_loop(0, x_count - 1, attend_inner, 0)
    attend(x_count - 1, True)

    def queries_left(n, carry):
        @pl.when(q_target(n) != me)
        def _():
            q_copy(n).wait_send()

        return carry

    lax.fori_loop(0, x_count * 4, queries_left, 0)
    send_blocks.wait_send()
    for copy in swap_copies():
        copy.wait_send()

    def join(state, columns):
        peak, total, summed = state
        sources = [lax.rem(x + k, x_count) * 4 + at_z for k in columns for at_z in range(4)]
        for source in sources:
            arrived(stat_in.at[source], stat_recv.at[source])
            arrived(o_in.at[source], o_recv.at[source])
        stats = [stat_in[source] for source in sources]
        new_peak = functools.reduce(jnp.maximum, [stat[0:1] for stat in stats], peak)
        decay = jnp.exp2(peak - new_peak)
        total, summed = total * decay, summed * decay
        for source, stat in zip(sources, stats):
            share = jnp.exp2(stat[0:1] - new_peak)
            total = total + share * stat[4:5]
            summed = summed + share * o_in[source].astype(F32)
        return new_peak, total, summed

    state = (
        jnp.full((1, pair), PEAK_FLOOR, F32),
        jnp.zeros((1, pair), F32),
        jnp.zeros((HD, pair), F32),
    )
    if x_count > 1:
        state = join(state, range(1, x_count))
    _, total, summed = join(state, range(1))
    joined = (summed / total).T.astype(BF16)
    attended[core] = jnp.concatenate([joined[:rows], joined[rows:]], axis=1)
    share_heads = pltpu.make_async_remote_copy(
        src_ref=attended.at[core],
        dst_ref=attended.at[core],
        send_sem=att_sem.at[0],
        recv_sem=att_sem.at[1],
        device_id={"kv": sibling},
        device_id_type=MESH,
    )
    share_heads.start()

    def spread(count, first, q):
        at = lax.broadcasted_iota(I32, (count, rows), 0)
        row = (at // 16) * 4 + ((at // 8) % 2) * 2 + at % 2 + first
        hit = (row == lax.broadcasted_iota(I32, (count, rows), 1)) & ((at // 2) % 4 == q)
        return jnp.where(hit, 1.0, 0.0).astype(BF16)

    def spread_heads(c):
        return [dot(spread(16 * chips, 0, q), attended[c]).astype(BF16) for q in range(4)]

    def project(c, parts, n):
        total = None
        for q in range(4):
            term = dot(parts[q], wo[c, :, pl.ds(q * lanes + n * strip, strip)])
            total = term if total is None else total + term
        return total

    steps = sorted(
        ((a, b) for a in range(x_count) for b in range(4) if (a, b) != (0, 0)),
        key=lambda ab: -min(ab[0], x_count - ab[0]) - min(ab[1], 4 - ab[1]),
    )

    def chip_at(n):
        return lax.rem(x + steps[n][0], x_count) * 4 + lax.rem(z + steps[n][1], 4)

    def rs_copy(n, k):
        to = chip_at(n)
        part = pl.ds(k * strip, strip)
        return pltpu.make_async_remote_copy(
            src_ref=rs_out.at[to, :, part],
            dst_ref=rs_in.at[chip, :, part],
            send_sem=rs_send.at[k, n],
            recv_sem=rs_recv.at[k, chip],
            device_id={"kv": to * 2 + core},
            device_id_type=MESH,
        )

    arrived(wo.at[core], own_sem.at[2 * x_count])
    parts = spread_heads(core)
    for k in range(strips):
        acc[:, pl.ds(k * strip, strip)] = project(core, parts, k)
    arrived(wo.at[other], kv_recv.at[2 * x_count])
    arrived(attended.at[other], att_sem.at[1])
    parts = spread_heads(other)
    for k in range(strips):
        part = pl.ds(k * strip, strip)
        term = acc[:, part] + project(other, parts, k)
        rs_out[:, :, part] = term.astype(BF16).reshape(chips, 16, strip)

        for n in range(len(steps)):
            rs_copy(n, k).start()

    def sums_left(i, carry):
        for p in range(4):

            @pl.when(o_target(head_at(i), p) != me)
            def _():
                for copy in o_copies(i, p):
                    copy.wait_send()

        return carry

    lax.fori_loop(0, x_count, sums_left, 0)
    share_heads.wait_send()

    results = []
    for k in range(strips):
        part = pl.ds(k * strip, strip)
        result = rs_out[chip, :, part].astype(F32)
        for q in range(4):
            start = core * half + q * lanes + k * strip
            own = hid[:, pl.ds(pl.multiple_of(start, strip), strip)]
            result = result + dot(spread(16, chip * 4, q), own)
        results.append(result)
    for k in range(strips):
        part = pl.ds(k * strip, strip)

        for n in reversed(range(len(steps))):
            source = chip_at(n)
            arrived(rs_in.at[source, :, part], rs_recv.at[k, source])
            results[k] = results[k] + rs_in[source, :, part].astype(F32)
    result = jnp.concatenate(results, axis=1)

    def fin_copy(c):
        return pltpu.make_async_remote_copy(
            src_ref=fin_out.at[c],
            dst_ref=fin_in.at[core],
            send_sem=fin_send.at[c],
            recv_sem=fin_recv.at[core],
            device_id={"section": after, "kv": chip * 2 + c},
            device_id_type=MESH,
        )

    for c in range(2):
        mine = result[8 * c : 8 * c + 8]
        fin_out[c] = jnp.concatenate(
            [mine[:, : lanes // 2], mine[:, lanes // 2 :]], axis=0
        ).astype(BF16)
        fin_copy(c).start()

    for k in range(strips):
        for n in range(len(steps)):
            rs_copy(n, k).wait_send()
    for c in range(2):
        arrived(fin_in.at[c], fin_recv.at[c])
    final = []
    for c in range(2):
        rows_in = fin_in[c].astype(F32)
        for q in range(4):
            for h in range(2):
                final.append(rows_in[h * 8 + q * 2 : h * 8 + q * 2 + 2])
    out[0] = jnp.concatenate(final, axis=1)
    for c in range(2):
        fin_copy(c).wait_send()


def local(sections, kv_count, *args):
    hidden, _, query_weight, key_cache = args[:4]
    rows, width = hidden.shape[1:]
    slots, block = key_cache.shape[1:3]
    x_count, chips = kv_count // 8, kv_count // 2
    pair, wide = 2 * rows, 8 * rows
    lanes = width // 8
    strips = 2
    pieces = 4
    dma = pltpu.SemaphoreType.DMA
    out = pl.pallas_call(
        functools.partial(kernel, sections, kv_count),
        out_shape=pltpu.VMEM((1, 2, width), F32),
        in_specs=[pl.BlockSpec(memory_space=pl.ANY)] * 9,
        out_specs=pl.BlockSpec(memory_space=pltpu.VMEM),
        scratch_shapes=[
            pltpu.SMEM(args[6].shape, I32),
            pltpu.SMEM(args[7].shape, I32),
            pltpu.SMEM(args[8].shape, I32),
            pltpu.VMEM((rows, width), BF16),
            pltpu.VMEM((1, width), F32),
            pltpu.VMEM((width, 2 * HD), BF16),
            pltpu.VMEM((x_count, 2 * slots, block, HD), BF16),
            pltpu.VMEM((x_count, 2 * slots, block, HD), BF16),
            pltpu.VMEM((2, 2 * HD, width // 2), BF16),
            pltpu.VMEM((x_count, wide, HD), BF16),
            pltpu.VMEM((wide, 128), BF16),
            pltpu.VMEM((2 * slots * block, 128), BF16),
            pltpu.VMEM((2, 16, 128), F32),
            pltpu.VMEM((2, slots * block, wide), F32),
            pltpu.VMEM((pair, HD), BF16),
            pltpu.VMEM((x_count, 4, HD, pair), BF16),
            pltpu.VMEM((x_count, 4, 8, pair), F32),
            pltpu.VMEM((chips, HD, pair), BF16),
            pltpu.VMEM((chips, 8, pair), F32),
            pltpu.VMEM((2, rows, 2 * HD), BF16),
            pltpu.VMEM((16 * chips, lanes), F32),
            pltpu.VMEM((chips, 16, lanes), BF16),
            pltpu.VMEM((chips, 16, lanes), BF16),
            pltpu.VMEM((2, 16, lanes // 2), BF16),
            pltpu.VMEM((2, 16, lanes // 2), BF16),
            dma((5,)),
            dma((pieces,)),
            dma((2 * x_count + 1,)),
            dma((2 * x_count + 1,)),
            dma((2 * x_count + 1,)),
            dma((2,)),
            dma((4 * x_count,)),
            dma((4 * x_count,)),
            dma((4 * x_count,)),
            dma((chips,)),
            dma((4 * x_count,)),
            dma((chips,)),
            dma((2,)),
            dma((strips, chips)),
            dma((strips, chips)),
            dma((2,)),
            dma((2,)),
        ],
        compiler_params=pltpu.CompilerParams(
            collective_id=0, has_side_effects=True, vmem_limit_bytes=60 << 20
        ),
        name="relay_attention",
    )(*args)
    return out.astype(BF16)


def solution(mesh):
    placed = (
        P("section", None, None),
        P("section", None),
        P("section", None, "kv"),
        P("section", "kv", None, None),
        P("section", "kv", None, None),
        P("section", "kv", None),
        P("kv"),
        P(),
        P(),
    )
    sections, kv_count = mesh.shape["section"], mesh.shape["kv"]
    return jax.shard_map(
        functools.partial(local, sections, kv_count),
        mesh=mesh,
        in_specs=placed,
        out_specs=P("section", "kv", None),
        check_vma=False,
    )
```

```python
import functools
import math

import jax
import jax.numpy as jnp
from jax import lax
from jax.experimental import pallas as pl
from jax.experimental.pallas import tpu as pltpu
from jax.sharding import PartitionSpec as P

HD = 128
LOG2_SCALE = math.log2(math.e) / math.sqrt(HD)
HIDDEN_BY_MASK = -1e30
PEAK_FLOOR = -1e28
MESH = pl.DeviceIdType.MESH
BF16, F32, I32 = jnp.bfloat16, jnp.float32, jnp.int32


def dot(a, b, contract=((1,), (0,))):
    return lax.dot_general(a, b, (contract, ((), ())), preferred_element_type=F32)


def arrived(ref, sem):
    pltpu.make_async_copy(ref, ref, sem).wait()


def kernel(
    sections,
    kv_count,
    hid_h,
    gain_h,
    wq_h,
    key_h,
    value_h,
    wo_h,
    block_pos_h,
    lengths_h,
    span_start_h,
    out,
    block_pos,
    lengths,
    span_start,
    hid,
    gain,
    wq,
    keys,
    values,
    wo,
    queries,
    onehot,
    bias,
    blocks,
    scores,
    q_out,
    o_out,
    stat_out,
    o_in,
    stat_in,
    attended,
    acc,
    rs_out,
    rs_in,
    fin_out,
    fin_in,
    in_sem,
    wq_sem,
    own_sem,
    kv_send,
    kv_recv,
    block_sem,
    q_send,
    q_recv,
    o_send,
    o_recv,
    stat_send,
    stat_recv,
    att_sem,
    rs_send,
    rs_recv,
    fin_send,
    fin_recv,
):
    rows, width = hid.shape
    x_count = kv_count // 8
    chips = kv_count // 2
    slots, block = key_h.shape[1], key_h.shape[2]
    half = width // 2
    lanes = rs_out.shape[2]
    strip = min(512, lanes)
    strips = lanes // strip
    span = slots * block
    wide = onehot.shape[0]
    pair = 2 * rows
    section = lax.axis_index("section")
    me = lax.axis_index("kv")
    chip = lax.div(me, 2)
    core = lax.rem(me, 2)
    other = 1 - core
    sibling = chip * 2 + other
    x = lax.div(chip, 4)
    z = lax.rem(chip, 4)
    side = lax.div(z, 2)
    place = core * 2 + lax.rem(z, 2)

    load_hid = pltpu.make_async_copy(hid_h.at[0], hid, in_sem.at[0])
    load_gain = pltpu.make_async_copy(gain_h, gain, in_sem.at[1])
    load_hid.start()
    load_gain.start()
    pieces = wq_sem.shape[0]
    deep = wq.shape[0] // pieces

    def load_wq(n):
        part = pl.ds(n * deep, deep)
        return pltpu.make_async_copy(wq_h.at[0, part], wq.at[part], wq_sem.at[n])

    for n in range(pieces):
        load_wq(n).start()
    scalar_loads = [
        pltpu.make_async_copy(src, dst, in_sem.at[2 + n])
        for n, (src, dst) in enumerate(
            ((block_pos_h, block_pos), (lengths_h, lengths), (span_start_h, span_start))
        )
    ]
    for load in scalar_loads:
        load.start()

    barrier = pltpu.get_barrier_semaphore()

    def greet(n, carry):
        @pl.when(n != me)
        def _():
            pl.semaphore_signal(barrier, inc=1, device_id={"kv": n}, device_id_type=MESH)

        return carry

    lax.fori_loop(0, kv_count, greet, 0)
    after = lax.rem(section + 1, sections)
    before = lax.rem(section + sections - 1, sections)
    for there in (after, before):
        for c in range(2):
            pl.semaphore_signal(
                barrier,
                inc=1,
                device_id={"section": there, "kv": chip * 2 + c},
                device_id_type=MESH,
            )

    load_hid.wait()
    load_gain.wait()
    step = min(1024, deep)
    squares = jnp.zeros((rows, 1), F32)
    for n in range(width // step):
        part = hid[:, n * step : (n + 1) * step].astype(F32)
        squares = squares + jnp.sum(part * part, axis=1, keepdims=True)
    scale = lax.rsqrt(squares / width + 1e-05)
    projected = jnp.zeros((rows, 2 * HD), F32)
    for n in range(width // step):
        if n * step % deep == 0:
            load_wq(n * step // deep).wait()
        part = pl.ds(n * step, step)
        normed = (hid[:, part].astype(F32) * scale * gain[:, part]).astype(BF16)
        projected = projected + dot(normed, wq[part, :])
    projected = projected * LOG2_SCALE
    q_out[pl.ds(0, rows), :] = projected[:, :HD].astype(BF16)
    q_out[pl.ds(rows, rows), :] = projected[:, HD:].astype(BF16)

    def moved(i, at_z):
        return lax.rem((i + 1) * jnp.where(lax.rem(at_z, 2) == 0, 1, x_count - 1), x_count)

    def head_at(i):
        return lax.rem(x + moved(i, z), x_count)

    def head_lanes(slot, c):
        return pl.ds(pl.multiple_of((slot * 2 + c) * HD, HD), HD)

    def own_copies():
        copies = []
        for i in range(x_count):
            slot = head_at(i)
            for k, (src, dst) in enumerate(((key_h, keys), (value_h, values))):
                copies.append(
                    pltpu.make_async_copy(
                        src.at[0, :, :, head_lanes(slot, core)],
                        dst.at[slot, pl.ds(0, slots)],
                        own_sem.at[i * 2 + k],
                    )
                )
        copies.append(
            pltpu.make_async_copy(
                wo_h.at[0, :, pl.ds(pl.multiple_of(core * half, half), half)],
                wo.at[core],
                own_sem.at[2 * x_count],
            )
        )
        return copies

    def to_sibling(src, dst, n, kind):
        return pltpu.make_async_remote_copy(
            src_ref=src,
            dst_ref=dst,
            send_sem=kv_send.at[kind],
            recv_sem=kv_recv.at[n],
            device_id={"kv": sibling},
            device_id_type=MESH,
        )

    def swap_copies():
        copies = []
        for i in range(x_count):
            slot = head_at(i)
            for k, (src, dst) in enumerate(((key_h, keys), (value_h, values))):
                copies.append(
                    to_sibling(
                        src.at[0, :, :, head_lanes(slot, other)],
                        dst.at[slot, pl.ds(slots, slots)],
                        i * 2 + k,
                        k,
                    )
                )
        copies.append(
            to_sibling(
                wo_h.at[0, :, pl.ds(pl.multiple_of(other * half, half), half)],
                wo.at[core],
                2 * x_count,
                2,
            )
        )
        return copies

    for copy in own_copies():
        copy.start()
    pl.semaphore_wait(barrier, kv_count - 1 + 4)

    def q_target(n):
        to_z = lax.rem(z + n, 4)
        to_x = lax.rem(x + x_count - moved(lax.div(n, 4), to_z), x_count)
        return to_x * 8 + to_z * 2 + side

    def q_place():
        return queries.at[x, pl.ds(pl.multiple_of(place * pair, pair), pair)]

    def q_copy(n):
        return pltpu.make_async_remote_copy(
            src_ref=q_out,
            dst_ref=q_place(),
            send_sem=q_send,
            recv_sem=q_recv.at[x],
            device_id={"kv": q_target(n)},
            device_id_type=MESH,
        )

    def send_queries(n, carry):
        @pl.when(q_target(n) != me)
        def _():
            q_copy(n).start()

        @pl.when(q_target(n) == me)
        def _():
            pltpu.make_async_copy(q_out, q_place(), q_recv.at[x]).start()

        return carry

    lax.fori_loop(0, 4, send_queries, 0)

    for load in scalar_loads:
        load.wait()
    blocks[0] = jnp.zeros((16, 128), F32)
    for j in range(slots):
        blocks[0, j : j + 1, :] = jnp.full((1, 128), block_pos[j], I32).astype(F32)
    send_blocks = pltpu.make_async_remote_copy(
        src_ref=blocks.at[0],
        dst_ref=blocks.at[1],
        send_sem=block_sem.at[0],
        recv_sem=block_sem.at[1],
        device_id={"kv": sibling},
        device_id_type=MESH,
    )
    send_blocks.start()
    for copy in swap_copies():
        copy.start()
    lane = lax.broadcasted_iota(I32, (1, 128), 1)
    prefill = rows - lengths.shape[0]
    limits = span_start[0] + lane + 1
    for r in range(lengths.shape[0]):
        limits = jnp.where(lane == prefill + r, lengths[r], limits)
    limits = limits.astype(F32)
    token = lax.broadcasted_iota(I32, (block, 128), 0).astype(F32)

    def mask_columns(which):
        for j in range(slots):
            position = blocks[which, j : j + 1, :] * float(block) + token
            bias[pl.ds((which * slots + j) * block, block), :] = jnp.where(
                position < limits, 0.0, HIDDEN_BY_MASK
            ).astype(BF16)

    mask_columns(0)
    onehot[...] = jnp.where(
        lax.rem(lax.broadcasted_iota(I32, (wide, 128), 0), rows)
        == lax.broadcasted_iota(I32, (wide, 128), 1),
        1.0,
        0.0,
    ).astype(BF16)
    arrived(blocks.at[1], block_sem.at[1])
    mask_columns(1)
    if x_count > 1:
        lax.fori_loop(4, 8, send_queries, 0)

    def o_target(slot, p):
        return slot * 8 + (core * 2 + p % 2) * 2 + p // 2

    def column_of(i):
        return jnp.where(i == x_count - 1, 1, 0)

    def o_copies(i, p):
        slot = head_at(i)
        return tuple(
            pltpu.make_async_remote_copy(
                src_ref=src.at[slot, p],
                dst_ref=dst.at[chip],
                send_sem=send,
                recv_sem=recv.at[column_of(i)],
                device_id={"kv": o_target(slot, p)},
                device_id_type=MESH,
            )
            for src, dst, send, recv in (
                (o_out, o_in, o_send, o_recv),
                (stat_out, stat_in, stat_send, stat_recv),
            )
        )

    def await_first(i):
        slot = head_at(i)
        arrived(queries.at[slot], q_recv.at[slot])
        arrived(keys.at[slot, pl.ds(0, slots)], own_sem.at[i * 2])

    def score(i, n):
        slot = head_at(i)
        query = jnp.concatenate([queries[slot], onehot[...]], axis=1)
        key = keys[slot, pl.ds(n * slots, slots)].reshape(span, HD)
        key = jnp.concatenate([key, bias[pl.ds(n * span, span), :]], axis=1)
        scores[n] = dot(key, query, ((1,), (1,)))

    def weigh(i, n, state, columns):
        peak, total, summed = state
        part = scores[n, :, columns].reshape(span // 8, 8, peak.shape[1])
        largest = jnp.max(jnp.max(part, axis=0), axis=0, keepdims=True)
        new_peak = jnp.maximum(peak, largest)
        decay = jnp.exp2(peak - new_peak)
        weights = jnp.exp2(part - new_peak[None])
        total = total * decay + jnp.sum(weights, axis=0)
        weights = weights.reshape(span, peak.shape[1]).astype(BF16)
        value = values[head_at(i), pl.ds(n * slots, slots)].reshape(span, HD)
        summed = summed * decay[0:1] + dot(value, weights, ((0,), (0,)))
        return new_peak, total, summed

    def attend(i, last):
        slot = head_at(i)
        arrived(values.at[slot, pl.ds(0, slots)], own_sem.at[i * 2 + 1])
        arrived(keys.at[slot, pl.ds(slots, slots)], kv_recv.at[i * 2])
        score(i, 1)
        state = (
            jnp.full((8, wide), PEAK_FLOOR, F32),
            jnp.zeros((8, wide), F32),
            jnp.zeros((HD, wide), F32),
        )
        state = weigh(i, 0, state, pl.ds(0, wide))
        arrived(values.at[slot, pl.ds(slots, slots)], kv_recv.at[i * 2 + 1])
        if not last:
            await_first(i + 1)
            score(i + 1, 0)
        cuts = 2 if last else 1
        for cut in range(cuts):
            size = wide // cuts
            columns = slice(cut * size, (cut + 1) * size)
            peak, total, summed = weigh(
                i, 1, [value[:, columns] for value in state], pl.ds(cut * size, size)
            )
            total = jnp.sum(total, axis=0, keepdims=True)
            owners = range(cut * 4 // cuts, (cut + 1) * 4 // cuts)
            for p in owners:
                part = slice(p * pair - cut * size, (p + 1) * pair - cut * size)
                o_out[slot, p] = summed[:, part].astype(BF16)
                stat_out[slot, p] = jnp.concatenate(
                    [peak[0:4, part], jnp.broadcast_to(total[:, part], (4, pair))], axis=0
                )
            for p in owners:

                @pl.when(o_target(slot, p) != me)
                def _():
                    for copy in o_copies(i, p):
                        copy.start()

                @pl.when(o_target(slot, p) == me)
                def _():
                    pltpu.make_async_copy(
                        o_out.at[slot, p], o_in.at[chip], o_recv.at[column_of(i)]
                    ).start()
                    pltpu.make_async_copy(
                        stat_out.at[slot, p], stat_in.at[chip], stat_recv.at[column_of(i)]
                    ).start()

    def attend_inner(i, carry):
        attend(i, False)
        return carry

    await_first(0)
    score(0, 0)
    if x_count > 2:
        lax.fori_loop(8, x_count * 4, send_queries, 0)
    lax.fori_loop(0, x_count - 1, attend_inner, 0)
    attend(x_count - 1, True)

    def left(ref, sem):
        @pl.when(side == core)
        def _():
            arrived(ref.at[pl.ds(0, chips - 1)], sem)

        @pl.when(side != core)
        def _():
            arrived(ref, sem)

    left(o_in, q_send)
    send_blocks.wait_send()
    arrived(keys.at[:, pl.ds(slots, slots)], kv_send.at[0])
    arrived(values.at[:, pl.ds(slots, slots)], kv_send.at[1])
    arrived(wo.at[core], kv_send.at[2])

    def join(state, columns):
        peak, total, summed = state
        sources = [lax.rem(x + k, x_count) * 4 + at_z for k in columns for at_z in range(4)]
        which = 1 if 0 in columns else 0
        arrived(stat_in.at[pl.ds(0, len(sources))], stat_recv.at[which])
        arrived(o_in.at[pl.ds(0, len(sources))], o_recv.at[which])
        stats = [stat_in[source] for source in sources]
        new_peak = functools.reduce(jnp.maximum, [stat[0:1] for stat in stats], peak)
        decay = jnp.exp2(peak - new_peak)
        total, summed = total * decay, summed * decay
        for source, stat in zip(sources, stats):
            share = jnp.exp2(stat[0:1] - new_peak)
            total = total + share * stat[4:5]
            summed = summed + share * o_in[source].astype(F32)
        return new_peak, total, summed

    state = (
        jnp.full((1, pair), PEAK_FLOOR, F32),
        jnp.zeros((1, pair), F32),
        jnp.zeros((HD, pair), F32),
    )
    if x_count > 1:
        state = join(state, range(1, x_count))
    _, total, summed = join(state, range(1))
    joined = (summed / total).T.astype(BF16)
    attended[core] = jnp.concatenate([joined[:rows], joined[rows:]], axis=1)
    share_heads = pltpu.make_async_remote_copy(
        src_ref=attended.at[core],
        dst_ref=attended.at[core],
        send_sem=att_sem.at[0],
        recv_sem=att_sem.at[1],
        device_id={"kv": sibling},
        device_id_type=MESH,
    )
    share_heads.start()

    def spread(count, first, q):
        at = lax.broadcasted_iota(I32, (count, rows), 0)
        row = (at // 16) * 4 + ((at // 8) % 2) * 2 + at % 2 + first
        hit = (row == lax.broadcasted_iota(I32, (count, rows), 1)) & ((at // 2) % 4 == q)
        return jnp.where(hit, 1.0, 0.0).astype(BF16)

    def spread_heads(c):
        return [dot(spread(16 * chips, 0, q), attended[c]).astype(BF16) for q in range(4)]

    def project(c, parts, n):
        total = None
        for q in range(4):
            term = dot(parts[q], wo[c, :, pl.ds(q * lanes + n * strip, strip)])
            total = term if total is None else total + term
        return total

    steps = sorted(
        ((a, b) for a in range(x_count) for b in range(4) if (a, b) != (0, 0)),
        key=lambda ab: -min(ab[0], x_count - ab[0]) - min(ab[1], 4 - ab[1]),
    )

    def chip_at(n):
        return lax.rem(x + steps[n][0], x_count) * 4 + lax.rem(z + steps[n][1], 4)

    def rs_copy(n):
        to = chip_at(n)
        return pltpu.make_async_remote_copy(
            src_ref=rs_out.at[to],
            dst_ref=rs_in.at[chip],
            send_sem=rs_send,
            recv_sem=rs_recv,
            device_id={"kv": to * 2 + core},
            device_id_type=MESH,
        )

    arrived(wo.at[core], own_sem.at[2 * x_count])
    parts = spread_heads(core)
    for k in range(strips):
        acc[:, pl.ds(k * strip, strip)] = project(core, parts, k)
    arrived(wo.at[other], kv_recv.at[2 * x_count])
    arrived(attended.at[other], att_sem.at[1])
    parts = spread_heads(other)
    for k in range(strips):
        part = pl.ds(k * strip, strip)
        term = acc[:, part] + project(other, parts, k)
        rs_out[:, :, part] = term.astype(BF16).reshape(chips, 16, strip)
    for n in range(len(steps)):
        rs_copy(n).start()

    left(o_in, o_send)
    left(stat_in, stat_send)
    share_heads.wait_send()

    results = []
    for k in range(strips):
        part = pl.ds(k * strip, strip)
        result = rs_out[chip, :, part].astype(F32)
        for q in range(4):
            start = core * half + q * lanes + k * strip
            own = hid[:, pl.ds(pl.multiple_of(start, strip), strip)]
            result = result + dot(spread(16, chip * 4, q), own)
        results.append(result)
    arrived(rs_in.at[pl.ds(0, chips - 1)], rs_recv)
    result = jnp.concatenate(results, axis=1)
    for n in range(len(steps)):
        result = result + rs_in[chip_at(n)].astype(F32)

    def fin_copy(c):
        return pltpu.make_async_remote_copy(
            src_ref=fin_out.at[c],
            dst_ref=fin_in.at[core],
            send_sem=fin_send,
            recv_sem=fin_recv,
            device_id={"section": after, "kv": chip * 2 + c},
            device_id_type=MESH,
        )

    for c in range(2):
        mine = result[8 * c : 8 * c + 8]
        fin_out[c] = jnp.concatenate(
            [mine[:, : lanes // 2], mine[:, lanes // 2 :]], axis=0
        ).astype(BF16)
        fin_copy(c).start()

    arrived(rs_in.at[pl.ds(0, chips - 1)], rs_send)
    arrived(fin_in, fin_recv)
    final = []
    for c in range(2):
        rows_in = fin_in[c].astype(F32)
        for q in range(4):
            for h in range(2):
                final.append(rows_in[h * 8 + q * 2 : h * 8 + q * 2 + 2])
    out[0] = jnp.concatenate(final, axis=1)
    arrived(fin_out, fin_send)


def local(sections, kv_count, *args):
    hidden, _, query_weight, key_cache = args[:4]
    rows, width = hidden.shape[1:]
    slots, block = key_cache.shape[1:3]
    x_count, chips = kv_count // 8, kv_count // 2
    pair, wide = 2 * rows, 8 * rows
    lanes = width // 8
    pieces = 4
    dma = pltpu.SemaphoreType.DMA
    out = pl.pallas_call(
        functools.partial(kernel, sections, kv_count),
        out_shape=pltpu.VMEM((1, 2, width), F32),
        in_specs=[pl.BlockSpec(memory_space=pl.ANY)] * 9,
        out_specs=pl.BlockSpec(memory_space=pltpu.VMEM),
        scratch_shapes=[
            pltpu.SMEM(args[6].shape, I32),
            pltpu.SMEM(args[7].shape, I32),
            pltpu.SMEM(args[8].shape, I32),
            pltpu.VMEM((rows, width), BF16),
            pltpu.VMEM((1, width), F32),
            pltpu.VMEM((width, 2 * HD), BF16),
            pltpu.VMEM((x_count, 2 * slots, block, HD), BF16),
            pltpu.VMEM((x_count, 2 * slots, block, HD), BF16),
            pltpu.VMEM((2, 2 * HD, width // 2), BF16),
            pltpu.VMEM((x_count, wide, HD), BF16),
            pltpu.VMEM((wide, 128), BF16),
            pltpu.VMEM((2 * slots * block, 128), BF16),
            pltpu.VMEM((2, 16, 128), F32),
            pltpu.VMEM((2, slots * block, wide), F32),
            pltpu.VMEM((pair, HD), BF16),
            pltpu.VMEM((x_count, 4, HD, pair), BF16),
            pltpu.VMEM((x_count, 4, 8, pair), F32),
            pltpu.VMEM((chips, HD, pair), BF16),
            pltpu.VMEM((chips, 8, pair), F32),
            pltpu.VMEM((2, rows, 2 * HD), BF16),
            pltpu.VMEM((16 * chips, lanes), F32),
            pltpu.VMEM((chips, 16, lanes), BF16),
            pltpu.VMEM((chips, 16, lanes), BF16),
            pltpu.VMEM((2, 16, lanes // 2), BF16),
            pltpu.VMEM((2, 16, lanes // 2), BF16),
            dma((5,)),
            dma((pieces,)),
            dma((2 * x_count + 1,)),
            dma((3,)),
            dma((2 * x_count + 1,)),
            dma((2,)),
            dma,
            dma((x_count,)),
            dma,
            dma((2,)),
            dma,
            dma((2,)),
            dma((2,)),
            dma,
            dma,
            dma,
            dma,
        ],
        compiler_params=pltpu.CompilerParams(
            collective_id=0, has_side_effects=True, vmem_limit_bytes=60 << 20
        ),
        name="relay_attention",
    )(*args)
    return out.astype(BF16)


def solution(mesh):
    placed = (
        P("section", None, None),
        P("section", None),
        P("section", None, "kv"),
        P("section", "kv", None, None),
        P("section", "kv", None, None),
        P("section", "kv", None),
        P("kv"),
        P(),
        P(),
    )
    sections, kv_count = mesh.shape["section"], mesh.shape["kv"]
    return jax.shard_map(
        functools.partial(local, sections, kv_count),
        mesh=mesh,
        in_specs=placed,
        out_specs=P("section", "kv", None),
        check_vma=False,
    )
```

```python
import functools
import math

import jax
import jax.numpy as jnp
from jax import lax
from jax.experimental import pallas as pl
from jax.experimental.pallas import tpu as pltpu
from jax.sharding import PartitionSpec as P

HD = 128
LOG2_SCALE = math.log2(math.e) / math.sqrt(HD)
HIDDEN_BY_MASK = -1e30
PEAK_FLOOR = -1e28
MESH = pl.DeviceIdType.MESH
BF16, F32, I32 = jnp.bfloat16, jnp.float32, jnp.int32


def dot(a, b, contract=((1,), (0,))):
    return lax.dot_general(a, b, (contract, ((), ())), preferred_element_type=F32)


def arrived(ref, sem):
    pltpu.make_async_copy(ref, ref, sem).wait()


def kernel(
    sections,
    kv_count,
    hid_h,
    gain_h,
    wq_h,
    key_h,
    value_h,
    wo_h,
    block_pos_h,
    lengths_h,
    span_start_h,
    out,
    block_pos,
    lengths,
    span_start,
    hid,
    gain,
    wq,
    keys,
    values,
    wo,
    queries,
    onehot,
    bias,
    blocks,
    scores,
    q_out,
    o_out,
    stat_out,
    o_in,
    stat_in,
    attended,
    acc,
    rs_out,
    rs_in,
    fin_out,
    fin_in,
    in_sem,
    wq_sem,
    own_sem,
    kv_send,
    kv_recv,
    block_sem,
    q_send,
    q_recv,
    o_send,
    o_recv,
    stat_send,
    stat_recv,
    att_sem,
    rs_send,
    rs_recv,
    fin_send,
    fin_recv,
):
    rows, width = hid.shape
    x_count = kv_count // 8
    chips = kv_count // 2
    slots, block = key_h.shape[1], key_h.shape[2]
    half = width // 2
    lanes = rs_out.shape[2]
    strip = min(512, lanes)
    strips = lanes // strip
    span = slots * block
    wide = onehot.shape[0]
    pair = 2 * rows
    section = lax.axis_index("section")
    me = lax.axis_index("kv")
    chip = lax.div(me, 2)
    core = lax.rem(me, 2)
    other = 1 - core
    sibling = chip * 2 + other
    x = lax.div(chip, 4)
    z = lax.rem(chip, 4)
    side = lax.div(z, 2)
    place = core * 2 + lax.rem(z, 2)

    load_hid = pltpu.make_async_copy(hid_h.at[0], hid, in_sem.at[0])
    load_gain = pltpu.make_async_copy(gain_h, gain, in_sem.at[1])
    load_hid.start()
    load_gain.start()
    pieces = wq_sem.shape[0]
    deep = wq.shape[0] // pieces

    def load_wq(n):
        part = pl.ds(n * deep, deep)
        return pltpu.make_async_copy(wq_h.at[0, part], wq.at[part], wq_sem.at[n])

    for n in range(pieces):
        load_wq(n).start()
    scalar_loads = [
        pltpu.make_async_copy(src, dst, in_sem.at[2 + n])
        for n, (src, dst) in enumerate(
            ((block_pos_h, block_pos), (lengths_h, lengths), (span_start_h, span_start))
        )
    ]
    for load in scalar_loads:
        load.start()

    barrier = pltpu.get_barrier_semaphore()

    def greet(n, carry):
        @pl.when(n != me)
        def _():
            pl.semaphore_signal(barrier, inc=1, device_id={"kv": n}, device_id_type=MESH)

        return carry

    lax.fori_loop(0, kv_count, greet, 0)
    after = lax.rem(section + 1, sections)
    before = lax.rem(section + sections - 1, sections)
    for there in (after, before):
        for c in range(2):
            pl.semaphore_signal(
                barrier,
                inc=1,
                device_id={"section": there, "kv": chip * 2 + c},
                device_id_type=MESH,
            )

    load_hid.wait()
    load_gain.wait()
    step = min(1024, deep)
    squares = jnp.zeros((rows, 1), F32)
    for n in range(width // step):
        part = hid[:, n * step : (n + 1) * step].astype(F32)
        squares = squares + jnp.sum(part * part, axis=1, keepdims=True)
    scale = lax.rsqrt(squares / width + 1e-05)
    projected = jnp.zeros((rows, 2 * HD), F32)
    for n in range(width // step):
        if n * step % deep == 0:
            load_wq(n * step // deep).wait()
        part = pl.ds(n * step, step)
        normed = (hid[:, part].astype(F32) * scale * gain[:, part]).astype(BF16)
        projected = projected + dot(normed, wq[part, :])
    projected = projected * LOG2_SCALE
    q_out[pl.ds(0, rows), :] = projected[:, :HD].astype(BF16)
    q_out[pl.ds(rows, rows), :] = projected[:, HD:].astype(BF16)

    def moved(i, at_z):
        return lax.rem((i + 1) * jnp.where(lax.rem(at_z, 2) == 0, 1, x_count - 1), x_count)

    def head_at(i):
        return lax.rem(x + moved(i, z), x_count)

    def head_lanes(slot, c):
        return pl.ds(pl.multiple_of((slot * 2 + c) * HD, HD), HD)

    def own_copies():
        copies = []
        for i in range(x_count):
            slot = head_at(i)
            for k, (src, dst) in enumerate(((key_h, keys), (value_h, values))):
                copies.append(
                    pltpu.make_async_copy(
                        src.at[0, :, :, head_lanes(slot, core)],
                        dst.at[slot, pl.ds(0, slots)],
                        own_sem.at[i * 2 + k],
                    )
                )
        copies.append(
            pltpu.make_async_copy(
                wo_h.at[0, :, pl.ds(pl.multiple_of(core * half, half), half)],
                wo.at[core],
                own_sem.at[2 * x_count],
            )
        )
        return copies

    def to_sibling(src, dst, n, kind):
        return pltpu.make_async_remote_copy(
            src_ref=src,
            dst_ref=dst,
            send_sem=kv_send.at[kind],
            recv_sem=kv_recv.at[n],
            device_id={"kv": sibling},
            device_id_type=MESH,
        )

    def swap_copies():
        copies = []
        for i in range(x_count):
            slot = head_at(i)
            for k, (src, dst) in enumerate(((key_h, keys), (value_h, values))):
                copies.append(
                    to_sibling(
                        src.at[0, :, :, head_lanes(slot, other)],
                        dst.at[slot, pl.ds(slots, slots)],
                        i * 2 + k,
                        k,
                    )
                )
        copies.append(
            to_sibling(
                wo_h.at[0, :, pl.ds(pl.multiple_of(other * half, half), half)],
                wo.at[core],
                2 * x_count,
                2,
            )
        )
        return copies

    pl.semaphore_wait(barrier, kv_count - 1 + 4)

    def q_target(n):
        to_z = lax.rem(z + 2 + 3 * n, 4)
        to_x = lax.rem(x + x_count - moved(lax.div(n, 4), to_z), x_count)
        return to_x * 8 + to_z * 2 + side

    def q_place():
        return queries.at[x, pl.ds(pl.multiple_of(place * pair, pair), pair)]

    def q_copy(n):
        return pltpu.make_async_remote_copy(
            src_ref=q_out,
            dst_ref=q_place(),
            send_sem=q_send,
            recv_sem=q_recv.at[x],
            device_id={"kv": q_target(n)},
            device_id_type=MESH,
        )

    def send_queries(n, carry):
        @pl.when(q_target(n) != me)
        def _():
            q_copy(n).start()

        @pl.when(q_target(n) == me)
        def _():
            pltpu.make_async_copy(q_out, q_place(), q_recv.at[x]).start()

        return carry

    lax.fori_loop(0, min(8, x_count * 4), send_queries, 0)

    for copy in own_copies():
        copy.start()

    for load in scalar_loads:
        load.wait()
    blocks[0] = jnp.zeros((16, 128), F32)
    for j in range(slots):
        blocks[0, j : j + 1, :] = jnp.full((1, 128), block_pos[j], I32).astype(F32)
    send_blocks = pltpu.make_async_remote_copy(
        src_ref=blocks.at[0],
        dst_ref=blocks.at[1],
        send_sem=block_sem.at[0],
        recv_sem=block_sem.at[1],
        device_id={"kv": sibling},
        device_id_type=MESH,
    )
    send_blocks.start()
    for copy in swap_copies():
        copy.start()
    lane = lax.broadcasted_iota(I32, (1, 128), 1)
    prefill = rows - lengths.shape[0]
    limits = span_start[0] + lane + 1
    for r in range(lengths.shape[0]):
        limits = jnp.where(lane == prefill + r, lengths[r], limits)
    limits = limits.astype(F32)
    token = lax.broadcasted_iota(I32, (block, 128), 0).astype(F32)

    def mask_columns(which):
        for j in range(slots):
            position = blocks[which, j : j + 1, :] * float(block) + token
            bias[pl.ds((which * slots + j) * block, block), :] = jnp.where(
                position < limits, 0.0, HIDDEN_BY_MASK
            ).astype(BF16)

    mask_columns(0)
    onehot[...] = jnp.where(
        lax.rem(lax.broadcasted_iota(I32, (wide, 128), 0), rows)
        == lax.broadcasted_iota(I32, (wide, 128), 1),
        1.0,
        0.0,
    ).astype(BF16)
    arrived(blocks.at[1], block_sem.at[1])
    mask_columns(1)

    def o_target(slot, p):
        return slot * 8 + (core * 2 + p % 2) * 2 + p // 2

    def column_of(i):
        return jnp.where(i == x_count - 1, 1, 0)

    def o_copies(i, p):
        slot = head_at(i)
        return tuple(
            pltpu.make_async_remote_copy(
                src_ref=src.at[slot, p],
                dst_ref=dst.at[chip],
                send_sem=send,
                recv_sem=recv.at[column_of(i)],
                device_id={"kv": o_target(slot, p)},
                device_id_type=MESH,
            )
            for src, dst, send, recv in (
                (o_out, o_in, o_send, o_recv),
                (stat_out, stat_in, stat_send, stat_recv),
            )
        )

    def await_first(i):
        slot = head_at(i)
        arrived(queries.at[slot], q_recv.at[slot])
        arrived(keys.at[slot, pl.ds(0, slots)], own_sem.at[i * 2])

    def score(i, n):
        slot = head_at(i)
        query = jnp.concatenate([queries[slot], onehot[...]], axis=1)
        key = keys[slot, pl.ds(n * slots, slots)].reshape(span, HD)
        key = jnp.concatenate([key, bias[pl.ds(n * span, span), :]], axis=1)
        scores[n] = dot(key, query, ((1,), (1,)))

    def weigh(i, n, state, columns):
        peak, total, summed = state
        part = scores[n, :, columns].reshape(span // 8, 8, peak.shape[1])
        largest = jnp.max(jnp.max(part, axis=0), axis=0, keepdims=True)
        new_peak = jnp.maximum(peak, largest)
        decay = jnp.exp2(peak - new_peak)
        weights = jnp.exp2(part - new_peak[None])
        total = total * decay + jnp.sum(weights, axis=0)
        weights = weights.reshape(span, peak.shape[1]).astype(BF16)
        value = values[head_at(i), pl.ds(n * slots, slots)].reshape(span, HD)
        summed = summed * decay[0:1] + dot(value, weights, ((0,), (0,)))
        return new_peak, total, summed

    def attend(i, last):
        slot = head_at(i)
        arrived(values.at[slot, pl.ds(0, slots)], own_sem.at[i * 2 + 1])
        arrived(keys.at[slot, pl.ds(slots, slots)], kv_recv.at[i * 2])
        arrived(values.at[slot, pl.ds(slots, slots)], kv_recv.at[i * 2 + 1])
        if not last:
            await_first(i + 1)
        score(i, 1)
        state = (
            jnp.full((8, wide), PEAK_FLOOR, F32),
            jnp.zeros((8, wide), F32),
            jnp.zeros((HD, wide), F32),
        )
        state = weigh(i, 0, state, pl.ds(0, wide))
        if not last:
            score(i + 1, 0)
        cuts = 2 if last else 1
        for cut in range(cuts):
            size = wide // cuts
            columns = slice(cut * size, (cut + 1) * size)
            peak, total, summed = weigh(
                i, 1, [value[:, columns] for value in state], pl.ds(cut * size, size)
            )
            total = jnp.sum(total, axis=0, keepdims=True)
            owners = range(cut * 4 // cuts, (cut + 1) * 4 // cuts)
            for p in owners:
                part = slice(p * pair - cut * size, (p + 1) * pair - cut * size)
                o_out[slot, p] = summed[:, part].astype(BF16)
                stat_out[slot, p] = jnp.concatenate(
                    [peak[0:4, part], jnp.broadcast_to(total[:, part], (4, pair))], axis=0
                )
            for p in owners:

                @pl.when(o_target(slot, p) != me)
                def _():
                    for copy in o_copies(i, p):
                        copy.start()

                @pl.when(o_target(slot, p) == me)
                def _():
                    pltpu.make_async_copy(
                        o_out.at[slot, p], o_in.at[chip], o_recv.at[column_of(i)]
                    ).start()
                    pltpu.make_async_copy(
                        stat_out.at[slot, p], stat_in.at[chip], stat_recv.at[column_of(i)]
                    ).start()

    def attend_inner(i, carry):
        attend(i, False)
        return carry

    await_first(0)
    score(0, 0)
    if x_count > 2:
        lax.fori_loop(8, x_count * 4, send_queries, 0)
    lax.fori_loop(0, x_count - 1, attend_inner, 0)
    attend(x_count - 1, True)

    def left(ref, sem):
        @pl.when(side == core)
        def _():
            arrived(ref.at[pl.ds(0, chips - 1)], sem)

        @pl.when(side != core)
        def _():
            arrived(ref, sem)


    arrived(wo.at[core], own_sem.at[2 * x_count])
    arrived(wo.at[other], kv_recv.at[2 * x_count])

    def join(state, columns):
        peak, total, summed = state
        sources = [lax.rem(x + k, x_count) * 4 + at_z for k in columns for at_z in range(4)]
        which = 1 if 0 in columns else 0
        arrived(stat_in.at[pl.ds(0, len(sources))], stat_recv.at[which])
        arrived(o_in.at[pl.ds(0, len(sources))], o_recv.at[which])
        stats = [stat_in[source] for source in sources]
        new_peak = functools.reduce(jnp.maximum, [stat[0:1] for stat in stats], peak)
        decay = jnp.exp2(peak - new_peak)
        total, summed = total * decay, summed * decay
        for source, stat in zip(sources, stats):
            share = jnp.exp2(stat[0:1] - new_peak)
            total = total + share * stat[4:5]
            summed = summed + share * o_in[source].astype(F32)
        return new_peak, total, summed

    state = (
        jnp.full((1, pair), PEAK_FLOOR, F32),
        jnp.zeros((1, pair), F32),
        jnp.zeros((HD, pair), F32),
    )
    if x_count > 1:
        state = join(state, range(1, x_count))
    _, total, summed = join(state, range(1))
    joined = (summed / total).T.astype(BF16)
    attended[core] = jnp.concatenate([joined[:rows], joined[rows:]], axis=1)
    share_heads = pltpu.make_async_remote_copy(
        src_ref=attended.at[core],
        dst_ref=attended.at[core],
        send_sem=att_sem.at[0],
        recv_sem=att_sem.at[1],
        device_id={"kv": sibling},
        device_id_type=MESH,
    )
    share_heads.start()

    def spread(count, first, q):
        at = lax.broadcasted_iota(I32, (count, rows), 0)
        row = (at // 16) * 4 + ((at // 8) % 2) * 2 + at % 2 + first
        hit = (row == lax.broadcasted_iota(I32, (count, rows), 1)) & ((at // 2) % 4 == q)
        return jnp.where(hit, 1.0, 0.0).astype(BF16)

    def spread_heads(c):
        return [dot(spread(16 * chips, 0, q), attended[c]).astype(BF16) for q in range(4)]

    def project(c, parts, n):
        total = None
        for q in range(4):
            term = dot(parts[q], wo[c, :, pl.ds(q * lanes + n * strip, strip)])
            total = term if total is None else total + term
        return total

    steps = sorted(
        ((a, b) for a in range(x_count) for b in range(4) if (a, b) != (0, 0)),
        key=lambda ab: -min(ab[0], x_count - ab[0]) - min(ab[1], 4 - ab[1]),
    )

    def chip_at(n):
        return lax.rem(x + steps[n][0], x_count) * 4 + lax.rem(z + steps[n][1], 4)

    def rs_copy(n, k):
        to = chip_at(n)
        part = pl.ds(k * strip, strip)
        return pltpu.make_async_remote_copy(
            src_ref=rs_out.at[to, :, part],
            dst_ref=rs_in.at[chip, :, part],
            send_sem=rs_send,
            recv_sem=rs_recv.at[k],
            device_id={"kv": to * 2 + core},
            device_id_type=MESH,
        )

    parts = spread_heads(core)
    for k in range(strips):
        acc[:, pl.ds(k * strip, strip)] = project(core, parts, k)
    arrived(attended.at[other], att_sem.at[1])
    parts = spread_heads(other)
    for k in range(strips):
        part = pl.ds(k * strip, strip)
        term = acc[:, part] + project(other, parts, k)
        rs_out[:, :, part] = term.astype(BF16).reshape(chips, 16, strip)
        for n in range(len(steps)):
            rs_copy(n, k).start()

    left(o_in, q_send)
    send_blocks.wait_send()
    arrived(keys.at[:, pl.ds(slots, slots)], kv_send.at[0])
    arrived(values.at[:, pl.ds(slots, slots)], kv_send.at[1])
    arrived(wo.at[core], kv_send.at[2])
    left(o_in, o_send)
    left(stat_in, stat_send)
    share_heads.wait_send()

    results = []
    for k in range(strips):
        part = pl.ds(k * strip, strip)
        result = rs_out[chip, :, part].astype(F32)
        for q in range(4):
            start = core * half + q * lanes + k * strip
            own = hid[:, pl.ds(pl.multiple_of(start, strip), strip)]
            result = result + dot(spread(16, chip * 4, q), own)
        results.append(result)
    for k in range(strips):
        arrived(rs_in.at[pl.ds(0, chips - 1), :, pl.ds(k * strip, strip)], rs_recv.at[k])
    result = jnp.concatenate(results, axis=1)
    for n in range(len(steps)):
        result = result + rs_in[chip_at(n)].astype(F32)

    def fin_copy(c):
        return pltpu.make_async_remote_copy(
            src_ref=fin_out.at[c],
            dst_ref=fin_in.at[core],
            send_sem=fin_send,
            recv_sem=fin_recv,
            device_id={"section": after, "kv": chip * 2 + c},
            device_id_type=MESH,
        )

    for c in range(2):
        mine = result[8 * c : 8 * c + 8]
        fin_out[c] = jnp.concatenate(
            [mine[:, : lanes // 2], mine[:, lanes // 2 :]], axis=0
        ).astype(BF16)
        fin_copy(c).start()

    arrived(rs_in.at[pl.ds(0, chips - 1)], rs_send)
    arrived(fin_in, fin_recv)
    final = []
    for c in range(2):
        rows_in = fin_in[c].astype(F32)
        for q in range(4):
            for h in range(2):
                final.append(rows_in[h * 8 + q * 2 : h * 8 + q * 2 + 2])
    out[0] = jnp.concatenate(final, axis=1)
    arrived(fin_out, fin_send)


def local(sections, kv_count, *args):
    hidden, _, query_weight, key_cache = args[:4]
    rows, width = hidden.shape[1:]
    slots, block = key_cache.shape[1:3]
    x_count, chips = kv_count // 8, kv_count // 2
    pair, wide = 2 * rows, 8 * rows
    lanes = width // 8
    pieces = 4
    dma = pltpu.SemaphoreType.DMA
    out = pl.pallas_call(
        functools.partial(kernel, sections, kv_count),
        out_shape=pltpu.VMEM((1, 2, width), F32),
        in_specs=[pl.BlockSpec(memory_space=pl.ANY)] * 9,
        out_specs=pl.BlockSpec(memory_space=pltpu.VMEM),
        scratch_shapes=[
            pltpu.SMEM(args[6].shape, I32),
            pltpu.SMEM(args[7].shape, I32),
            pltpu.SMEM(args[8].shape, I32),
            pltpu.VMEM((rows, width), BF16),
            pltpu.VMEM((1, width), F32),
            pltpu.VMEM((width, 2 * HD), BF16),
            pltpu.VMEM((x_count, 2 * slots, block, HD), BF16),
            pltpu.VMEM((x_count, 2 * slots, block, HD), BF16),
            pltpu.VMEM((2, 2 * HD, width // 2), BF16),
            pltpu.VMEM((x_count, wide, HD), BF16),
            pltpu.VMEM((wide, 128), BF16),
            pltpu.VMEM((2 * slots * block, 128), BF16),
            pltpu.VMEM((2, 16, 128), F32),
            pltpu.VMEM((2, slots * block, wide), F32),
            pltpu.VMEM((pair, HD), BF16),
            pltpu.VMEM((x_count, 4, HD, pair), BF16),
            pltpu.VMEM((x_count, 4, 8, pair), F32),
            pltpu.VMEM((chips, HD, pair), BF16),
            pltpu.VMEM((chips, 8, pair), F32),
            pltpu.VMEM((2, rows, 2 * HD), BF16),
            pltpu.VMEM((16 * chips, lanes), F32),
            pltpu.VMEM((chips, 16, lanes), BF16),
            pltpu.VMEM((chips, 16, lanes), BF16),
            pltpu.VMEM((2, 16, lanes // 2), BF16),
            pltpu.VMEM((2, 16, lanes // 2), BF16),
            dma((5,)),
            dma((pieces,)),
            dma((2 * x_count + 1,)),
            dma((3,)),
            dma((2 * x_count + 1,)),
            dma((2,)),
            dma,
            dma((x_count,)),
            dma,
            dma((2,)),
            dma,
            dma((2,)),
            dma((2,)),
            dma,
            dma((max(1, lanes // 512),)),
            dma,
            dma,
        ],
        compiler_params=pltpu.CompilerParams(
            collective_id=0, has_side_effects=True, vmem_limit_bytes=60 << 20
        ),
        name="relay_attention",
    )(*args)
    return out.astype(BF16)


def solution(mesh):
    placed = (
        P("section", None, None),
        P("section", None),
        P("section", None, "kv"),
        P("section", "kv", None, None),
        P("section", "kv", None, None),
        P("section", "kv", None),
        P("kv"),
        P(),
        P(),
    )
    sections, kv_count = mesh.shape["section"], mesh.shape["kv"]
    return jax.shard_map(
        functools.partial(local, sections, kv_count),
        mesh=mesh,
        in_specs=placed,
        out_specs=P("section", "kv", None),
        check_vma=False,
    )
```
